32 devices in a mesh: dom: 8 (over y, x, core), blk: 4 (over z).
Axes of the slice: x: 2, y: 2, z: 4, core: 2. Of those that a mesh axis runs over, the one named last changes fastest.
Arguments:
- features: bfloat16 [32768, 128], P(('dom', 'blk')), may hold values from -6 to 6
- tile_vals: bfloat16 [2304, 128, 128], P(('dom', 'blk')), may hold values from -0.25 to 0.25
- tile_rows: int32 [32, 72], P(('dom', 'blk')), may hold values from 0 to 7
- tile_cols: int32 [32, 72], P(('dom', 'blk')), may hold values from 0 to 7
- tile_count: int32 [32, 4], P(('dom', 'blk')), may hold values from 1 to 18, as said below
- cut_weights: bfloat16 [32768, 384], P(('dom', 'blk')), may hold values from -0.4375 to 0.4375
- send_idx: int32 [32, 384], P(('dom', 'blk')), may hold values from 0 to 1023
- send_count: int32 [32, 8], P(('dom', 'blk')), may hold values from 0 to 48, as said below
- weight: bfloat16 [128, 256], replicated, may hold values from -0.5 to 0.5
- bias: float32 [256], replicated, may hold values from -3 to 3
- cotangent: bfloat16 [32768, 256], P(('dom', 'blk')), may hold values from -6 to 6
Outputs:
- out_y: bfloat16 [32768, 256], P(('dom', 'blk'))
- grad_x: bfloat16 [32768, 128], P(('dom', 'blk'))
- grad_w: float32 [128, 256], replicated
- grad_b: float32 [256], replicated
The draws below stay inside these ranges and needn't reach their ends.
Inputs may be any that keep to these rules, and one draw needn't show every extreme that they name: `tile_count`: every device has a source position with exactly 18 live slots; devices differ strongly in their counts. `send_count`: zero toward a device's own group; at each index along blk some group receives exactly 48 rows from every other group.
All inputs are finite; a program needn't handle non-finite values.
Results may differ from the reference program's by a relative error of at most 0.018.
Values may be sent and summed in bfloat16 or wider, within the bound.
A program may use at most 128 MiB of HBM per device.

```python
import math
import jax
import jax.numpy as jnp
from jax import lax

F = 128
H = 256
TILE = 128
ROWS_DEV = 1024
MAXT = 18
SENDMAX = 48
NODES = 32768
N_DOM = 8
N_BLK = 4


def draw_tile_count(key, part):
    keys = jax.random.split(key, 4)
    device_total = N_DOM * N_BLK
    heavy_flag = jax.random.randint(keys[0], (device_total, 1), 0, 4) == 0
    heavy = jax.random.randint(keys[1], (device_total, N_BLK), MAXT // 2, MAXT + 1)
    light = jax.random.randint(keys[2], (device_total, N_BLK), 1, MAXT // 2 + 1)
    counts = jnp.where(heavy_flag, heavy, light)
    fullest = jax.random.randint(keys[3], (device_total, 1), 0, N_BLK)
    counts = jnp.where(jnp.arange(N_BLK)[None, :] == fullest, MAXT, counts)
    return counts.astype(jnp.int32)


def draw_send_count(key, part):
    keys = jax.random.split(key, 2)
    base = jax.random.randint(keys[0], (N_DOM, N_BLK, N_DOM), 0, SENDMAX + 1)
    target = jax.random.randint(keys[1], (1, N_BLK, 1), 0, N_DOM)
    dest = jnp.arange(N_DOM)[None, None, :]
    anchor = jnp.arange(N_DOM)[:, None, None]
    counts = jnp.where(dest == target, SENDMAX, base)
    counts = jnp.where(dest == anchor, 0, counts)
    return counts.reshape(N_DOM * N_BLK, N_DOM).astype(jnp.int32)


def plant(values, key, least, largest):
    place = [jax.random.randint(jax.random.fold_in(key, axis), (), 0, length) for axis, length in enumerate(values.shape)]
    longest = values.shape.index(max(values.shape))
    neighbour = place[:longest] + [(place[longest] + 1) % values.shape[longest]] + place[longest + 1:]
    return values.at[tuple(place)].set(least).at[tuple(neighbour)].set(largest)


def levels(rng, shape, pieces, low, high):
    loudness = 1.0
    for dim, parts in pieces:
        steps = jax.random.uniform(jax.random.fold_in(jax.random.fold_in(rng, 6), dim), (parts,), jnp.float32, low / len(pieces), high / len(pieces))
        loudness = loudness * jnp.repeat(jnp.exp(steps), shape[dim] // parts).reshape((-1,) + (1,) * (len(shape) - 1 - dim))
    return loudness


def normal_values(stream_key, dims, deviation, most, cuts=(), held_as=jnp.bfloat16):
    factor_of = levels(stream_key, dims, cuts, -0.22, 0.18) if cuts else 1.0
    result = jax.random.normal(stream_key, dims, jnp.float32) * deviation * factor_of
    return jnp.minimum(jnp.maximum(result, -most), most).astype(held_as)


def setup_inputs(seed: int = 0) -> dict:
    splits = jax.random.split(jax.random.key(seed), 12)
    features = normal_values(splits[0], (NODES, F), 1.0, 6.0, ((0, 32),))
    tile_vals = normal_values(splits[1], (N_DOM * N_BLK * N_BLK * MAXT, TILE, TILE), (N_BLK * MAXT * TILE * TILE // (2 * ROWS_DEV)) ** -0.5, 0.25, ((0, 32),))
    tile_rows = plant(jax.random.randint(splits[2], (N_DOM * N_BLK, N_BLK * MAXT), 0, ROWS_DEV // TILE), jax.random.fold_in(splits[2], 1), 0, (ROWS_DEV // TILE) - 1).astype(jnp.int32)
    tile_cols = plant(jax.random.randint(splits[3], (N_DOM * N_BLK, N_BLK * MAXT), 0, ROWS_DEV // TILE), jax.random.fold_in(splits[3], 1), 0, (ROWS_DEV // TILE) - 1).astype(jnp.int32)
    tile_count = draw_tile_count(jax.random.fold_in(splits[11], 71), 0)
    cut_weights = normal_values(splits[5], (NODES, N_DOM * SENDMAX), (N_DOM * SENDMAX // 2) ** -0.5, 0.4375, ((0, 32),))
    send_idx = plant(jax.random.randint(splits[6], (N_DOM * N_BLK, N_DOM * SENDMAX), 0, ROWS_DEV), jax.random.fold_in(splits[6], 1), 0, ROWS_DEV - 1).astype(jnp.int32)
    send_count = draw_send_count(jax.random.fold_in(splits[11], 71), 0)
    weight = normal_values(splits[8], (F, H), F ** -0.5, 0.5)
    bias = normal_values(splits[9], (H,), 0.5, 3.0, (), jnp.float32)
    cotangent = normal_values(splits[10], (NODES, H), 1.0, 6.0, ((0, 32),))
    return {"features": features, "tile_vals": tile_vals, "tile_rows": tile_rows, "tile_cols": tile_cols, "tile_count": tile_count, "cut_weights": cut_weights, "send_idx": send_idx, "send_count": send_count, "weight": weight, "bias": bias, "cotangent": cotangent}


def reference(features, tile_vals, tile_rows, tile_cols, tile_count, cut_weights, send_idx, send_count, weight, bias, cotangent):
    device_total = N_DOM * N_BLK
    row_blocks = ROWS_DEV // TILE
    group_rows = N_BLK * ROWS_DEV
    step_ids = jnp.arange(N_BLK, dtype=jnp.int32)
    slot_ids = jnp.arange(MAXT, dtype=jnp.int32)
    limit_ids = jnp.arange(SENDMAX, dtype=jnp.int32)
    group_ids = jnp.arange(N_DOM, dtype=jnp.int32)
    scale = 1.0 / math.sqrt(NODES)

    def forward(device):
        group_idx = device // N_BLK
        position = device % N_BLK
        tiles = lax.dynamic_slice_in_dim(tile_vals, device * N_BLK * MAXT, N_BLK * MAXT, 0).astype(jnp.float32)
        tiles = tiles.reshape(N_BLK, MAXT, TILE, TILE)
        rows_here = tile_rows[device].reshape(N_BLK, MAXT)
        cols_here = tile_cols[device].reshape(N_BLK, MAXT)
        live = slot_ids[None, :] < tile_count[device][:, None]
        panels = lax.dynamic_slice_in_dim(features, group_idx * group_rows, group_rows, 0)
        panels = panels.reshape(N_BLK, row_blocks, TILE, F)
        source = (position - step_ids) % N_BLK
        picked = panels[source[:, None], cols_here].astype(jnp.float32)
        product = jnp.einsum('stij,stjf->stif', tiles, picked)
        product = jnp.where(live[:, :, None, None], product, 0.0)
        intra = jax.ops.segment_sum(product.reshape(N_BLK * MAXT, TILE, F), rows_here.reshape(-1), num_segments=row_blocks)
        intra = intra.reshape(ROWS_DEV, F)
        sources = group_ids * N_BLK + position
        chosen = lax.dynamic_slice_in_dim(send_idx[sources], group_idx * SENDMAX, SENDMAX, 1)
        values = features[sources[:, None] * ROWS_DEV + chosen]
        sent_live = limit_ids[None, :] < send_count[sources, group_idx][:, None]
        received = jnp.where(sent_live[:, :, None], values, jnp.zeros_like(values)).reshape(N_DOM * SENDMAX, F)
        own_cut = lax.dynamic_slice_in_dim(cut_weights, device * ROWS_DEV, ROWS_DEV, 0)
        aggregated = (intra + jnp.dot(own_cut, received, preferred_element_type=jnp.float32)).astype(jnp.bfloat16)
        pre = jnp.dot(aggregated, weight, preferred_element_type=jnp.float32) + bias
        sig = jax.nn.sigmoid(pre)
        out_rows = (pre * sig).astype(jnp.bfloat16)
        own_cot = lax.dynamic_slice_in_dim(cotangent, device * ROWS_DEV, ROWS_DEV, 0)
        dpre = (own_cot.astype(jnp.float32) * sig * (1.0 + pre * (1.0 - sig))).astype(jnp.bfloat16)
        weight_term = jnp.dot(aggregated.T, dpre, preferred_element_type=jnp.float32)
        bias_term = lax.optimization_barrier(jnp.sum(dpre.astype(jnp.float32), axis=0))
        dz_rows = jnp.dot(dpre, weight.T, preferred_element_type=jnp.float32).astype(jnp.bfloat16)
        cut_back = jnp.dot(own_cut.T, dz_rows, preferred_element_type=jnp.float32).astype(jnp.bfloat16)
        return (out_rows, dz_rows, cut_back, weight_term, bias_term)
    out_all, dz_all, back_all, weight_terms, bias_terms = lax.map(forward, jnp.arange(device_total, dtype=jnp.int32))

    def backward(device):
        group_idx = device // N_BLK
        position = device % N_BLK
        senders = group_idx * N_BLK + step_ids
        step_of = (step_ids - position) % N_BLK
        first = (senders * N_BLK + step_of) * MAXT
        tiles = tile_vals[first[:, None] + slot_ids[None, :]].astype(jnp.float32)
        flat = step_of[:, None] * MAXT + slot_ids[None, :]
        rows_here = tile_rows[senders[:, None], flat]
        cols_here = tile_cols[senders[:, None], flat]
        live = slot_ids[None, :] < tile_count[senders, step_of][:, None]
        dz_source = dz_all[senders].reshape(N_BLK, row_blocks, TILE, F)
        picked = dz_source[step_ids[:, None], rows_here].astype(jnp.float32)
        product = jnp.einsum('btji,btjf->btif', tiles, picked)
        product = jnp.where(live[:, :, None, None], product, 0.0)
        intra = jax.ops.segment_sum(product.reshape(N_BLK * MAXT, TILE, F), cols_here.reshape(-1), num_segments=row_blocks)
        intra = intra.reshape(ROWS_DEV, F)
        receivers = group_ids * N_BLK + position
        returned = lax.dynamic_slice_in_dim(back_all[receivers], group_idx * SENDMAX, SENDMAX, 1)
        sent_live = limit_ids[None, :] < send_count[device][:, None]
        returned = jnp.where(sent_live[:, :, None], returned.astype(jnp.float32), 0.0)
        cut_grad = jnp.zeros((ROWS_DEV, F), jnp.float32).at[send_idx[device]].add(returned.reshape(N_DOM * SENDMAX, F))
        return (intra + cut_grad).astype(jnp.bfloat16)
    grad_all = lax.map(backward, jnp.arange(device_total, dtype=jnp.int32))
    grad_w = lax.optimization_barrier(jnp.sum(weight_terms, axis=0)) * scale
    grad_b = lax.optimization_barrier(jnp.sum(bias_terms, axis=0)) * scale
    return (out_all.reshape(NODES, H), grad_all.reshape(NODES, F), grad_w, grad_b)
```

```python
import functools
import math

import jax
import jax.numpy as jnp
from jax import lax
from jax.experimental import pallas as pl
from jax.experimental.pallas import tpu as pltpu
from jax.sharding import PartitionSpec as P

MESH = pl.DeviceIdType.MESH
F32 = jnp.float32
BF16 = jnp.bfloat16


def dot(a, b, ca=1, cb=0):
    return lax.dot_general(a, b, (((ca,), (cb,)), ((), ())), preferred_element_type=F32)


def build(counts, rows, cols, send_counts, tiles, send_idx, x, a, picks, outgoing):
    step = pl.program_id(0)
    slots, side, _ = tiles.shape
    dom, most, width = outgoing.shape
    a[...] = jnp.zeros_like(a)

    def add(t, carry):
        r = pl.multiple_of(rows[0, step * slots + t] * side, side)
        c = pl.multiple_of(cols[0, step * slots + t] * side, side)
        a[0, pl.ds(r, side), pl.ds(c, side)] += tiles[t]
        return carry

    lax.fori_loop(0, counts[0, step], add, 0)

    @pl.when(step == 0)
    def _():
        lane = lax.broadcasted_iota(jnp.int32, send_idx.shape, 1)
        index = jnp.full(send_idx.shape, -1, jnp.int32)
        for k in range(dom):
            live = (lane >= k * most) & (lane < k * most + send_counts[0, k])
            index = jnp.where(live, send_idx[...], index)
        row = lax.broadcasted_iota(jnp.int32, picks.shape, 0)
        picks[...] = jnp.where(row == index, 1.0, 0.0).astype(BF16)
        outgoing[...] = dot(picks[...], x[...], 0, 0).astype(BF16).reshape(dom, most, width)


def layer(
    dom, blk, scale,
    a_hbm, x, cut, picks, outgoing, weight, bias, cot,
    y, grad_x, grad_w, grad_b,
    a, panels, received, back, returned, part, part_in, agg, dpre,
    w_out, w_in, w_mid, w_blk, w_all,
    a_sem, xs, xr, cs, cr, bs, br, ps, pr, w1s, w1r, w2s, w2r, w3s, w3r,
):
    g = lax.axis_index("dom")
    b = lax.axis_index("blk")
    rows, width = x.shape
    hidden = weight.shape[1]
    cuts = cut.shape[1]
    share = width // dom

    def load(s):
        return pltpu.make_async_copy(a_hbm.at[s], a.at[s], a_sem.at[s])

    for s in range(blk):
        load(s).start()

    def other(me, n, i):
        return lax.rem(me + i, n)

    barrier = pltpu.get_barrier_semaphore()

    @pl.loop(1, dom)
    def _(i):
        pl.semaphore_signal(barrier, inc=1, device_id=(other(g, dom, i), b), device_id_type=MESH)

    @pl.loop(1, blk)
    def _(i):
        pl.semaphore_signal(barrier, inc=1, device_id=(g, other(b, blk, i)), device_id_type=MESH)

    pl.semaphore_wait(barrier, dom + blk - 2)

    def over_dom(src, dst, ss, rs, peer, slot):
        return pltpu.make_async_remote_copy(
            src, dst, ss.at[peer], rs.at[slot], device_id=(peer, b), device_id_type=MESH
        )

    def over_blk(src, dst, ss, rs, peer, slot):
        return pltpu.make_async_remote_copy(
            src, dst, ss.at[peer], rs.at[slot], device_id=(g, peer), device_id_type=MESH
        )

    def each(n, me, body):
        @pl.loop(1, n)
        def _(i):
            body(other(me, n, i))

    each(blk, b, lambda k: over_blk(x, panels.at[b], xs, xr, k, b).start())
    each(dom, g, lambda k: over_dom(outgoing.at[k], received.at[g], cs, cr, k, g).start())
    received[g] = outgoing[g]

    load(0).wait()
    total = dot(a[0], x[...])
    each(dom, g, lambda k: over_dom(outgoing.at[k], received.at[k], cs, cr, k, k).wait_recv())
    total = total + dot(cut[...], received[...].reshape(cuts, width))

    def gather(s, acc):
        q = lax.rem(b - s + blk, blk)
        over_blk(x, panels.at[q], xs, xr, q, q).wait_recv()
        load(s).wait()
        return acc + dot(a[s], panels[q])

    total = lax.fori_loop(1, blk, gather, total)
    agg[...] = total.astype(BF16)
    bias_sum = jnp.zeros((1, hidden), F32)
    block = 256
    for n in range(rows // block):
        here = pl.ds(n * block, block)
        pre = dot(agg[here, :], weight[...]) + bias[...]
        s = 1.0 / (1.0 + jnp.exp(-pre))
        y[here, :] = (pre * s).astype(BF16)
        d = (cot[here, :].astype(F32) * s * (1.0 + pre * (1.0 - s))).astype(BF16)
        dpre[here, :] = d
        bias_sum = bias_sum + jnp.sum(d.astype(F32), axis=0, keepdims=True)

    dz_t = dot(weight[...], dpre[...], 1, 1).astype(BF16)
    back[...] = dot(dz_t, cut[...]).T.astype(BF16).reshape(back.shape)
    each(dom, g, lambda k: over_dom(back.at[k], returned.at[g], bs, br, k, g).start())
    returned[g] = back[g]

    w_term = dot(agg[...], dpre[...], 0, 0)
    w_out[:, :share, :] = w_term.reshape(dom, share, hidden)
    w_out[:, share:, :] = jnp.broadcast_to(bias_sum[None], (dom, 8, hidden))
    each(dom, g, lambda k: over_dom(w_out.at[k], w_in.at[g], w1s, w1r, k, g).start())
    w_in[g] = w_out[g]

    def spread(i, carry):
        q = lax.rem(b - i + blk, blk)
        part[q] = dot(dz_t, a[i]).astype(BF16)
        over_blk(part.at[q], part_in.at[b], ps, pr, q, b).start()
        return carry

    lax.fori_loop(1, blk, spread, 0)
    mine = dot(dz_t, a[0])

    each(dom, g, lambda k: over_dom(w_out.at[k], w_in.at[k], w1s, w1r, k, k).wait_recv())
    w_mid[...] = jnp.sum(w_in[...], axis=0)
    each(blk, b, lambda k: over_blk(w_mid, w_blk.at[b], w2s, w2r, k, b).start())
    w_blk[b] = w_mid[...]
    each(dom, g, lambda k: over_dom(back.at[k], returned.at[k], bs, br, k, k).wait_recv())
    from_cut = dot(picks[...], returned[...].reshape(cuts, width))
    each(blk, b, lambda k: over_blk(w_mid, w_blk.at[k], w2s, w2r, k, k).wait_recv())
    w_all[g] = jnp.sum(w_blk[...], axis=0) * scale
    each(dom, g, lambda k: over_dom(w_all.at[g], w_all.at[g], w3s, w3r, k, g).start())

    def collect(i, acc):
        q = lax.rem(b + i, blk)
        over_blk(part.at[q], part_in.at[q], ps, pr, q, q).wait_recv()
        return acc + part_in[q].astype(F32)

    mine = lax.fori_loop(1, blk, collect, mine)
    grad_x[...] = (mine.T + from_cut).astype(BF16)

    each(dom, g, lambda k: over_dom(w_all.at[k], w_all.at[k], w3s, w3r, k, k).wait_recv())
    grad_w[...] = w_all[:, :share, :].reshape(width, hidden)
    grad_b[...] = w_all[g, pl.ds(share, 1), :]

    each(blk, b, lambda k: over_blk(x, panels.at[b], xs, xr, k, b).wait_send())
    each(dom, g, lambda k: over_dom(outgoing.at[k], received.at[g], cs, cr, k, g).wait_send())
    each(dom, g, lambda k: over_dom(back.at[k], returned.at[g], bs, br, k, g).wait_send())
    each(dom, g, lambda k: over_dom(w_out.at[k], w_in.at[g], w1s, w1r, k, g).wait_send())
    each(blk, b, lambda k: over_blk(part.at[k], part_in.at[b], ps, pr, k, b).wait_send())
    each(blk, b, lambda k: over_blk(w_mid, w_blk.at[b], w2s, w2r, k, b).wait_send())
    each(dom, g, lambda k: over_dom(w_all.at[g], w_all.at[g], w3s, w3r, k, g).wait_send())


def shards(
    features, tile_vals, tile_rows, tile_cols, tile_count, cut_weights,
    send_idx, send_count, weight, bias, cotangent,
):
    rows, width = features.shape
    side = tile_vals.shape[1]
    blk = lax.axis_size("blk")
    dom = lax.axis_size("dom")
    slots = tile_vals.shape[0] // blk
    cuts = send_idx.shape[1]
    most = cuts // dom
    hidden = weight.shape[1]
    smem = pl.BlockSpec(memory_space=pltpu.SMEM)
    vmem = pl.BlockSpec(memory_space=pltpu.VMEM)
    whole = lambda *shape: pl.BlockSpec(shape, lambda s: (0,) * len(shape))
    a, picks, outgoing = pl.pallas_call(
        build,
        grid=(blk,),
        out_shape=(
            jax.ShapeDtypeStruct((blk, rows, rows), BF16),
            jax.ShapeDtypeStruct((rows, cuts), BF16),
            jax.ShapeDtypeStruct((dom, most, width), BF16),
        ),
        in_specs=[smem, smem, smem, smem,
                  pl.BlockSpec((slots, side, side), lambda s: (s, 0, 0)),
                  whole(1, cuts), whole(rows, width)],
        out_specs=(pl.BlockSpec((1, rows, rows), lambda s: (s, 0, 0)),
                   whole(rows, cuts), whole(dom, most, width)),
        compiler_params=pltpu.CompilerParams(vmem_limit_bytes=40 << 20),
    )(tile_count, tile_rows, tile_cols, send_count, tile_vals, send_idx, features)

    share = width // dom
    piece = share + 8
    dma = pltpu.SemaphoreType.DMA
    over_d, over_b = dma((dom,)), dma((blk,))
    y, grad_x, grad_w, grad_b = pl.pallas_call(
        functools.partial(layer, dom, blk, 1.0 / math.sqrt(dom * blk * rows)),
        out_shape=(
            jax.ShapeDtypeStruct((rows, hidden), BF16),
            jax.ShapeDtypeStruct((rows, width), BF16),
            jax.ShapeDtypeStruct((width, hidden), F32),
            jax.ShapeDtypeStruct((1, hidden), F32),
        ),
        in_specs=[pl.BlockSpec(memory_space=pl.ANY)] + [vmem] * 7,
        out_specs=(vmem,) * 4,
        scratch_shapes=[
            pltpu.VMEM((blk, rows, rows), BF16),
            pltpu.VMEM((blk, rows, width), BF16),
            pltpu.VMEM((dom, most, width), BF16),
            pltpu.VMEM((dom, most, width), BF16),
            pltpu.VMEM((dom, most, width), BF16),
            pltpu.VMEM((blk, width, rows), BF16),
            pltpu.VMEM((blk, width, rows), BF16),
            pltpu.VMEM((rows, width), BF16),
            pltpu.VMEM((rows, hidden), BF16),
            pltpu.VMEM((dom, piece, hidden), F32),
            pltpu.VMEM((dom, piece, hidden), F32),
            pltpu.VMEM((piece, hidden), F32),
            pltpu.VMEM((blk, piece, hidden), F32),
            pltpu.VMEM((dom, piece, hidden), F32),
            over_b, over_b, over_b, over_d, over_d, over_d, over_d,
            over_b, over_b, over_d, over_d, over_b, over_b, over_d, over_d,
        ],
        compiler_params=pltpu.CompilerParams(
            collective_id=0, has_side_effects=True, vmem_limit_bytes=60 << 20
        ),
    )(a, features, cut_weights, picks, outgoing, weight, bias.reshape(1, hidden), cotangent)
    return y, grad_x, grad_w, grad_b.reshape(hidden)


def solution(mesh):
    split = P(("dom", "blk"), None)
    in_specs = (
        split, P(("dom", "blk"), None, None), split, split, split, split, split, split,
        P(), P(), split,
    )
    out_specs = (split, split, P(), P())
    return jax.shard_map(shards, mesh=mesh, in_specs=in_specs, out_specs=out_specs, check_vma=False)
```

```python
import functools
import math

import jax
import jax.numpy as jnp
from jax import lax
from jax.experimental import pallas as pl
from jax.experimental.pallas import tpu as pltpu
from jax.sharding import PartitionSpec as P

MESH = pl.DeviceIdType.MESH
F32 = jnp.float32
BF16 = jnp.bfloat16


def dot(a, b, ca=1, cb=0):
    return lax.dot_general(a, b, (((ca,), (cb,)), ((), ())), preferred_element_type=F32)


def build(counts, rows, cols, send_counts, tiles, send_idx, x, a, picks, outgoing):
    step = pl.program_id(0)
    slots, side, _ = tiles.shape
    dom, most, width = outgoing.shape
    a[...] = jnp.zeros_like(a)

    def add(t, carry):
        r = pl.multiple_of(rows[0, step * slots + t] * side, side)
        c = pl.multiple_of(cols[0, step * slots + t] * side, side)
        a[0, pl.ds(r, side), pl.ds(c, side)] += tiles[t]
        return carry

    lax.fori_loop(0, counts[0, step], add, 0)

    @pl.when(step == 0)
    def _():
        lane = lax.broadcasted_iota(jnp.int32, send_idx.shape, 1)
        index = jnp.full(send_idx.shape, -1, jnp.int32)
        for k in range(dom):
            live = (lane >= k * most) & (lane < k * most + send_counts[0, k])
            index = jnp.where(live, send_idx[...], index)
        row = lax.broadcasted_iota(jnp.int32, picks.shape, 0)
        picks[...] = jnp.where(row == index, 1.0, 0.0).astype(BF16)
        outgoing[...] = dot(picks[...], x[...], 0, 0).astype(BF16).reshape(dom, most, width)


def layer(
    dom, blk, scale,
    a_hbm, x, cut_hbm, picks_hbm, outgoing, weight_hbm, bias, cot_hbm,
    y, grad_x, grad_w, grad_b,
    a, cut, picks, weight, cot,
    panels, received, back, returned, part, from_low, from_high, total, agg, dpre,
    w_out, w_in, w_mid, w_blk, w_all,
    a_sem, o_sem, up_s, up_r, dn_s, dn_r, cs, cr, bs, br,
    pu_s, pu_r, pd_s, pd_r, w1s, w1r, w2s, w2r, w3s, w3r,
):
    g = lax.axis_index("dom")
    b = lax.axis_index("blk")
    rows, width = x.shape
    hidden = weight.shape[1]
    cuts = cut.shape[1]
    share = width // dom
    last = blk - 1

    def load(s):
        return pltpu.make_async_copy(a_hbm.at[s], a.at[s], a_sem.at[s])

    operands = [
        pltpu.make_async_copy(src, dst, o_sem.at[n])
        for n, (src, dst) in enumerate(
            ((cut_hbm, cut), (weight_hbm, weight), (cot_hbm, cot), (picks_hbm, picks))
        )
    ]
    load(0).start()
    operands[0].start()
    for s in range(1, blk):
        load(s).start()
    for copy in operands[1:]:
        copy.start()

    def other(me, n, i):
        return lax.rem(me + i, n)

    barrier = pltpu.get_barrier_semaphore()

    @pl.loop(1, dom)
    def _(i):
        pl.semaphore_signal(barrier, inc=1, device_id=(other(g, dom, i), b), device_id_type=MESH)

    @pl.loop(1, blk)
    def _(i):
        pl.semaphore_signal(barrier, inc=1, device_id=(g, other(b, blk, i)), device_id_type=MESH)

    pl.semaphore_wait(barrier, dom + blk - 2)

    def over_dom(src, dst, ss, rs, peer, slot):
        return pltpu.make_async_remote_copy(
            src, dst, ss.at[peer], rs.at[slot], device_id=(peer, b), device_id_type=MESH
        )

    def over_blk(src, dst, ss, rs, peer, send, slot):
        return pltpu.make_async_remote_copy(
            src, dst, ss.at[send], rs.at[slot], device_id=(g, peer), device_id_type=MESH
        )

    def each(n, me, body):
        @pl.loop(1, n)
        def _(i):
            body(other(me, n, i))

    def up(q):
        return over_blk(panels.at[q], panels.at[q], up_s, up_r, jnp.minimum(b + 1, last), q, q)

    def down(q):
        return over_blk(panels.at[q], panels.at[q], dn_s, dn_r, jnp.maximum(b - 1, 0), q, q)

    panels[b] = x[...]
    pl.when(b < last)(lambda: up(b).start())
    pl.when(b > 0)(lambda: down(b).start())
    each(dom, g, lambda k: over_dom(outgoing.at[k], received.at[g], cs, cr, k, g).start())
    received[g] = outgoing[g]

    load(0).wait()
    total[...] = dot(a[0], x[...])
    operands[0].wait()
    each(dom, g, lambda k: over_dom(outgoing.at[k], received.at[k], cs, cr, k, k).wait_recv())
    total[...] += dot(cut[...], received[...].reshape(cuts, width))

    for s in range(1, blk):
        load(s).wait()

    @pl.loop(1, blk)
    def _(r):
        low, high = b - r, b + r

        @pl.when(low >= 0)
        def _():
            up(low).wait_recv()
            pl.when(b < last)(lambda: up(low).start())

        @pl.when(high <= last)
        def _():
            down(high).wait_recv()
            pl.when(b > 0)(lambda: down(high).start())

        @pl.when(low >= 0)
        def _():
            total[...] += dot(a[r], panels[low])

        @pl.when(high <= last)
        def _():
            total[...] += dot(a[blk - r], panels[high])

    agg[...] = total[...].astype(BF16)
    for copy in operands[1:]:
        copy.wait()
    bias_sum = jnp.zeros((1, hidden), F32)
    block = 256
    for n in range(rows // block):
        here = pl.ds(n * block, block)
        pre = dot(agg[here, :], weight[...]) + bias[...]
        s = 1.0 / (1.0 + jnp.exp(-pre))
        y[here, :] = (pre * s).astype(BF16)
        d = (cot[here, :].astype(F32) * s * (1.0 + pre * (1.0 - s))).astype(BF16)
        dpre[here, :] = d
        bias_sum = bias_sum + jnp.sum(d.astype(F32), axis=0, keepdims=True)

    dz_t = dot(weight[...], dpre[...], 1, 1).astype(BF16)

    def to_high(q):
        return over_blk(part.at[q], from_low.at[q], pu_s, pu_r, jnp.minimum(b + 1, last), q, q)

    def to_low(q):
        return over_blk(part.at[q], from_high.at[q], pd_s, pd_r, jnp.maximum(b - 1, 0), q, q)

    def relay(t):
        high = last - t + b
        low = t - last + b

        @pl.when((t >= b) & (high > b))
        def _():
            term = dot(dz_t, a[b - high + blk])

            @pl.when(b > 0)
            def _():
                to_high(high).wait_recv()
                part[high] = (term + from_low[high].astype(F32)).astype(BF16)

            @pl.when(b == 0)
            def _():
                part[high] = term.astype(BF16)

            to_high(high).start()

        @pl.when((low >= 0) & (low < b))
        def _():
            term = dot(dz_t, a[b - low])

            @pl.when(b < last)
            def _():
                to_low(low).wait_recv()
                part[low] = (term + from_high[low].astype(F32)).astype(BF16)

            @pl.when(b == last)
            def _():
                part[low] = term.astype(BF16)

            to_low(low).start()

    relay(0)

    back[...] = dot(dz_t, cut[...]).T.astype(BF16).reshape(back.shape)
    each(dom, g, lambda k: over_dom(back.at[k], returned.at[g], bs, br, k, g).start())
    returned[g] = back[g]

    w_term = dot(agg[...], dpre[...], 0, 0)
    w_out[:, :share, :] = w_term.reshape(dom, share, hidden)
    w_out[:, share:, :] = jnp.broadcast_to(bias_sum[None], (dom, 8, hidden))
    each(dom, g, lambda k: over_dom(w_out.at[k], w_in.at[g], w1s, w1r, k, g).start())
    w_in[g] = w_out[g]

    mine = dot(dz_t, a[0])

    def share_w(peer, slot):
        return over_blk(w_mid, w_blk.at[slot], w2s, w2r, peer, peer, slot)

    pl.loop(1, max(last - 1, 1))(relay)
    each(dom, g, lambda k: over_dom(w_out.at[k], w_in.at[k], w1s, w1r, k, k).wait_recv())
    w_mid[...] = jnp.sum(w_in[...], axis=0)
    each(blk, b, lambda k: share_w(k, b).start())
    w_blk[b] = w_mid[...]
    pl.loop(max(last - 1, 1), last)(relay)

    each(dom, g, lambda k: over_dom(back.at[k], returned.at[k], bs, br, k, k).wait_recv())
    from_cut = dot(picks[...], returned[...].reshape(cuts, width))
    each(blk, b, lambda k: share_w(k, k).wait_recv())
    w_all[g] = jnp.sum(w_blk[...], axis=0) * scale
    each(dom, g, lambda k: over_dom(w_all.at[g], w_all.at[g], w3s, w3r, k, g).start())

    grad = mine.T + from_cut
    total[...] = grad

    @pl.when(b > 0)
    def _():
        to_high(b).wait_recv()
        total[...] += from_low[b].astype(F32).T

    @pl.when(b < last)
    def _():
        to_low(b).wait_recv()
        total[...] += from_high[b].astype(F32).T

    grad_x[...] = total[...].astype(BF16)

    each(dom, g, lambda k: over_dom(w_all.at[k], w_all.at[k], w3s, w3r, k, k).wait_recv())
    grad_w[...] = w_all[:, :share, :].reshape(width, hidden)
    grad_b[...] = w_all[g, pl.ds(share, 1), :]

    @pl.loop(0, blk)
    def _(q):
        pl.when((b < last) & (q <= b))(lambda: up(q).wait_send())
        pl.when((b > 0) & (q >= b))(lambda: down(q).wait_send())
        pl.when(q > b)(lambda: to_high(q).wait_send())
        pl.when(q < b)(lambda: to_low(q).wait_send())

    each(dom, g, lambda k: over_dom(outgoing.at[k], received.at[g], cs, cr, k, g).wait_send())
    each(dom, g, lambda k: over_dom(back.at[k], returned.at[g], bs, br, k, g).wait_send())
    each(dom, g, lambda k: over_dom(w_out.at[k], w_in.at[g], w1s, w1r, k, g).wait_send())
    each(blk, b, lambda k: share_w(k, b).wait_send())
    each(dom, g, lambda k: over_dom(w_all.at[g], w_all.at[g], w3s, w3r, k, g).wait_send())


def deliver(*refs):
    count = len(refs) // 2
    sems = refs[-1]
    copies = [
        pltpu.make_async_copy(refs[n], refs[count + n], sems.at[n]) for n in range(count)
    ]
    for copy in copies:
        copy.start()
    for copy in copies:
        copy.wait()


def shards(
    features, tile_vals, tile_rows, tile_cols, tile_count, cut_weights,
    send_idx, send_count, weight, bias, cotangent,
):
    rows, width = features.shape
    side = tile_vals.shape[1]
    blk = lax.axis_size("blk")
    dom = lax.axis_size("dom")
    slots = tile_vals.shape[0] // blk
    cuts = send_idx.shape[1]
    most = cuts // dom
    hidden = weight.shape[1]
    smem = pl.BlockSpec(memory_space=pltpu.SMEM)
    vmem = pl.BlockSpec(memory_space=pltpu.VMEM)
    whole = lambda *shape: pl.BlockSpec(shape, lambda s: (0,) * len(shape))
    a, picks, outgoing = pl.pallas_call(
        build,
        grid=(blk,),
        out_shape=(
            jax.ShapeDtypeStruct((blk, rows, rows), BF16),
            jax.ShapeDtypeStruct((rows, cuts), BF16),
            jax.ShapeDtypeStruct((dom, most, width), BF16),
        ),
        in_specs=[smem, smem, smem, smem,
                  pl.BlockSpec((slots, side, side), lambda s: (s, 0, 0)),
                  whole(1, cuts), whole(rows, width)],
        out_specs=(pl.BlockSpec((1, rows, rows), lambda s: (s, 0, 0)),
                   whole(rows, cuts), whole(dom, most, width)),
        compiler_params=pltpu.CompilerParams(vmem_limit_bytes=60 << 20),
    )(tile_count, tile_rows, tile_cols, send_count, tile_vals, send_idx, features)

    share = width // dom
    piece = share + 8
    dma = pltpu.SemaphoreType.DMA
    over_d, over_b = dma((dom,)), dma((blk,))
    hbm = pl.BlockSpec(memory_space=pl.ANY)
    shapes = (
        jax.ShapeDtypeStruct((rows, hidden), BF16),
        jax.ShapeDtypeStruct((rows, width), BF16),
        jax.ShapeDtypeStruct((width, hidden), F32),
        jax.ShapeDtypeStruct((1, hidden), F32),
    )
    results = pl.pallas_call(
        functools.partial(layer, dom, blk, 1.0 / math.sqrt(dom * blk * rows)),
        out_shape=shapes,
        in_specs=[hbm, vmem, hbm, hbm, vmem, hbm, vmem, hbm],
        out_specs=(vmem,) * 4,
        scratch_shapes=[
            pltpu.VMEM((blk, rows, rows), BF16),
            pltpu.VMEM((rows, cuts), BF16),
            pltpu.VMEM((rows, cuts), BF16),
            pltpu.VMEM((width, hidden), BF16),
            pltpu.VMEM((rows, hidden), BF16),
            pltpu.VMEM((blk, rows, width), BF16),
            pltpu.VMEM((dom, most, width), BF16),
            pltpu.VMEM((dom, most, width), BF16),
            pltpu.VMEM((dom, most, width), BF16),
            pltpu.VMEM((blk, width, rows), BF16),
            pltpu.VMEM((blk, width, rows), BF16),
            pltpu.VMEM((blk, width, rows), BF16),
            pltpu.VMEM((rows, width), F32),
            pltpu.VMEM((rows, width), BF16),
            pltpu.VMEM((rows, hidden), BF16),
            pltpu.VMEM((dom, piece, hidden), F32),
            pltpu.VMEM((dom, piece, hidden), F32),
            pltpu.VMEM((piece, hidden), F32),
            pltpu.VMEM((blk, piece, hidden), F32),
            pltpu.VMEM((dom, piece, hidden), F32),
            over_b, dma((4,)), over_b, over_b, over_b, over_b, over_d, over_d, over_d, over_d,
            over_b, over_b, over_b, over_b, over_d, over_d, over_b, over_b, over_d, over_d,
        ],
        compiler_params=pltpu.CompilerParams(
            collective_id=0, has_side_effects=True, vmem_limit_bytes=60 << 20
        ),
    )(a, features, cut_weights, picks, outgoing, weight, bias.reshape(1, hidden), cotangent)
    y, grad_x, grad_w, grad_b = pl.pallas_call(
        deliver,
        out_shape=shapes,
        in_specs=[hbm] * 4,
        out_specs=(hbm,) * 4,
        scratch_shapes=[dma((4,))],
    )(*results)
    return y, grad_x, grad_w, grad_b.reshape(hidden)


def solution(mesh):
    split = P(("dom", "blk"), None)
    in_specs = (
        split, P(("dom", "blk"), None, None), split, split, split, split, split, split,
        P(), P(), split,
    )
    out_specs = (split, split, P(), P())
    return jax.shard_map(shards, mesh=mesh, in_specs=in_specs, out_specs=out_specs, check_vma=False)
```

```python
import functools
import math

import jax
import jax.numpy as jnp
from jax import lax
from jax.experimental import pallas as pl
from jax.experimental.pallas import tpu as pltpu
from jax.sharding import PartitionSpec as P

MESH = pl.DeviceIdType.MESH
F32 = jnp.float32
BF16 = jnp.bfloat16


def dot(a, b, ca=1, cb=0):
    return lax.dot_general(a, b, (((ca,), (cb,)), ((), ())), preferred_element_type=F32)


def build(counts, rows, cols, send_counts, tiles, send_idx, x, a, picks, outgoing):
    step = pl.program_id(0)
    slots, side, _ = tiles.shape
    dom, most, width = outgoing.shape
    a[...] = jnp.zeros_like(a)

    def add(t, carry):
        r = pl.multiple_of(rows[0, step * slots + t] * side, side)
        c = pl.multiple_of(cols[0, step * slots + t] * side, side)
        a[0, pl.ds(r, side), pl.ds(c, side)] += tiles[t]
        return carry

    lax.fori_loop(0, counts[0, step], add, 0)

    @pl.when(step == 0)
    def _():
        lane = lax.broadcasted_iota(jnp.int32, send_idx.shape, 1)
        index = jnp.full(send_idx.shape, -1, jnp.int32)
        for k in range(dom):
            live = (lane >= k * most) & (lane < k * most + send_counts[0, k])
            index = jnp.where(live, send_idx[...], index)
        row = lax.broadcasted_iota(jnp.int32, picks.shape, 0)
        picks[...] = jnp.where(row == index, 1.0, 0.0).astype(BF16)
        outgoing[...] = dot(picks[...], x[...], 0, 0).astype(BF16).reshape(dom, most, width)


def layer(
    dom, blk, scale,
    a_hbm, x, cut_hbm, picks_hbm, outgoing, weight_hbm, bias, cot_hbm,
    y, grad_x, grad_w, grad_b,
    a, cut, picks, weight, cot,
    panels, received, back, returned, part, from_low, from_high, total, agg, dpre,
    w_out, w_in, w_mid, w_blk, w_all,
    a_sem, o_sem, up_s, up_r, dn_s, dn_r, cs, cr, bs, br,
    pu_s, pu_r, pd_s, pd_r, w1s, w1r, w2s, w2r, w3s, w3r,
):
    g = lax.axis_index("dom")
    b = lax.axis_index("blk")
    rows, width = x.shape
    hidden = weight.shape[1]
    cuts = cut.shape[1]
    share = width // dom
    last = blk - 1

    def load(s):
        return pltpu.make_async_copy(a_hbm.at[s], a.at[s], a_sem.at[s])

    operands = [
        pltpu.make_async_copy(src, dst, o_sem.at[n])
        for n, (src, dst) in enumerate(
            ((cut_hbm, cut), (weight_hbm, weight), (cot_hbm, cot), (picks_hbm, picks))
        )
    ]
    load(0).start()
    operands[0].start()
    for s in range(1, blk):
        load(s).start()
    for copy in operands[1:]:
        copy.start()

    def other(me, n, i):
        return lax.rem(me + i, n)

    barrier = pltpu.get_barrier_semaphore()

    @pl.loop(1, dom)
    def _(i):
        pl.semaphore_signal(barrier, inc=1, device_id=(other(g, dom, i), b), device_id_type=MESH)

    @pl.loop(1, blk)
    def _(i):
        pl.semaphore_signal(barrier, inc=1, device_id=(g, other(b, blk, i)), device_id_type=MESH)

    pl.semaphore_wait(barrier, dom + blk - 2)

    def over_dom(src, dst, ss, rs, peer, slot):
        return pltpu.make_async_remote_copy(
            src, dst, ss.at[peer], rs.at[slot], device_id=(peer, b), device_id_type=MESH
        )

    def over_blk(src, dst, ss, rs, peer, send, slot):
        return pltpu.make_async_remote_copy(
            src, dst, ss.at[send], rs.at[slot], device_id=(g, peer), device_id_type=MESH
        )

    def each(n, me, body):
        @pl.loop(1, n)
        def _(i):
            body(other(me, n, i))

    def up(q):
        return over_blk(panels.at[q], panels.at[q], up_s, up_r, jnp.minimum(b + 1, last), q, q)

    def down(q):
        return over_blk(panels.at[q], panels.at[q], dn_s, dn_r, jnp.maximum(b - 1, 0), q, q)

    panels[b] = x[...]
    pl.when(b < last)(lambda: up(b).start())
    pl.when(b > 0)(lambda: down(b).start())
    each(dom, g, lambda k: over_dom(outgoing.at[k], received.at[g], cs, cr, k, g).start())
    received[g] = outgoing[g]

    load(0).wait()
    total[...] = dot(a[0], x[...])
    operands[0].wait()
    each(dom, g, lambda k: over_dom(outgoing.at[k], received.at[k], cs, cr, k, k).wait_recv())
    total[...] += dot(cut[...], received[...].reshape(cuts, width))

    for s in range(1, blk):
        load(s).wait()

    @pl.loop(1, blk)
    def _(r):
        low, high = b - r, b + r

        @pl.when(low >= 0)
        def _():
            up(low).wait_recv()
            pl.when(b < last)(lambda: up(low).start())

        @pl.when(high <= last)
        def _():
            down(high).wait_recv()
            pl.when(b > 0)(lambda: down(high).start())

        @pl.when(low >= 0)
        def _():
            total[...] += dot(a[r], panels[low])

        @pl.when(high <= last)
        def _():
            total[...] += dot(a[blk - r], panels[high])

    agg[...] = total[...].astype(BF16)
    for copy in operands[1:]:
        copy.wait()
    bias_sum = jnp.zeros((1, hidden), F32)
    block = 256
    for n in range(rows // block):
        here = pl.ds(n * block, block)
        pre = dot(agg[here, :], weight[...]) + bias[...]
        s = 1.0 / (1.0 + jnp.exp(-pre))
        y[here, :] = (pre * s).astype(BF16)
        d = (cot[here, :].astype(F32) * s * (1.0 + pre * (1.0 - s))).astype(BF16)
        dpre[here, :] = d
        bias_sum = bias_sum + jnp.sum(d.astype(F32), axis=0, keepdims=True)

    dz_t = dot(weight[...], dpre[...], 1, 1).astype(BF16)

    def to_high(q):
        return over_blk(part.at[q], from_low.at[q], pu_s, pu_r, jnp.minimum(b + 1, last), q, q)

    def to_low(q):
        return over_blk(part.at[q], from_high.at[q], pd_s, pd_r, jnp.maximum(b - 1, 0), q, q)

    def relay(t):
        high = last - t + b
        low = t - last + b

        @pl.when((t >= b) & (high > b))
        def _():
            term = dot(dz_t, a[b - high + blk])

            @pl.when(b > 0)
            def _():
                to_high(high).wait_recv()
                part[high] = (term + from_low[high].astype(F32)).astype(BF16)

            @pl.when(b == 0)
            def _():
                part[high] = term.astype(BF16)

            to_high(high).start()

        @pl.when((low >= 0) & (low < b))
        def _():
            term = dot(dz_t, a[b - low])

            @pl.when(b < last)
            def _():
                to_low(low).wait_recv()
                part[low] = (term + from_high[low].astype(F32)).astype(BF16)

            @pl.when(b == last)
            def _():
                part[low] = term.astype(BF16)

            to_low(low).start()

    relay(0)

    back[...] = dot(dz_t, cut[...]).T.astype(BF16).reshape(back.shape)
    each(dom, g, lambda k: over_dom(back.at[k], returned.at[g], bs, br, k, g).start())
    returned[g] = back[g]

    w_term = dot(agg[...], dpre[...], 0, 0)
    w_out[:, :share, :] = w_term.reshape(dom, share, hidden)
    w_out[:, share:, :] = jnp.broadcast_to(bias_sum[None], (dom, 8, hidden))
    each(dom, g, lambda k: over_dom(w_out.at[k], w_in.at[g], w1s, w1r, k, g).start())
    w_in[g] = w_out[g]

    mine = dot(dz_t, a[0])

    def share_w(peer, slot):
        return over_blk(w_mid, w_blk.at[slot], w2s, w2r, peer, peer, slot)

    each(dom, g, lambda k: over_dom(w_out.at[k], w_in.at[k], w1s, w1r, k, k).wait_recv())
    w_mid[...] = jnp.sum(w_in[...], axis=0)
    each(blk, b, lambda k: share_w(k, b).start())
    w_blk[b] = w_mid[...]
    pl.loop(1, min(2, last))(relay)

    each(blk, b, lambda k: share_w(k, k).wait_recv())
    w_all[g] = jnp.sum(w_blk[...], axis=0) * scale
    each(dom, g, lambda k: over_dom(w_all.at[g], w_all.at[g], w3s, w3r, k, g).start())
    pl.loop(2, last)(relay)

    each(dom, g, lambda k: over_dom(back.at[k], returned.at[k], bs, br, k, k).wait_recv())
    from_cut = dot(picks[...], returned[...].reshape(cuts, width))
    total[...] = mine.T + from_cut
    each(dom, g, lambda k: over_dom(w_all.at[k], w_all.at[k], w3s, w3r, k, k).wait_recv())
    grad_w[...] = w_all[:, :share, :].reshape(width, hidden)
    grad_b[...] = w_all[g, pl.ds(share, 1), :]

    @pl.when(b > 0)
    def _():
        to_high(b).wait_recv()
        total[...] += from_low[b].astype(F32).T

    @pl.when(b < last)
    def _():
        to_low(b).wait_recv()
        total[...] += from_high[b].astype(F32).T

    grad_x[...] = total[...].astype(BF16)

    @pl.loop(0, blk)
    def _(q):
        pl.when((b < last) & (q <= b))(lambda: up(q).wait_send())
        pl.when((b > 0) & (q >= b))(lambda: down(q).wait_send())
        pl.when(q > b)(lambda: to_high(q).wait_send())
        pl.when(q < b)(lambda: to_low(q).wait_send())

    each(dom, g, lambda k: over_dom(outgoing.at[k], received.at[g], cs, cr, k, g).wait_send())
    each(dom, g, lambda k: over_dom(back.at[k], returned.at[g], bs, br, k, g).wait_send())
    each(dom, g, lambda k: over_dom(w_out.at[k], w_in.at[g], w1s, w1r, k, g).wait_send())
    each(blk, b, lambda k: share_w(k, b).wait_send())
    each(dom, g, lambda k: over_dom(w_all.at[g], w_all.at[g], w3s, w3r, k, g).wait_send())


def deliver(*refs):
    count = len(refs) // 2
    for n in range(count):
        refs[count + n][...] = refs[n][...]


def shards(
    features, tile_vals, tile_rows, tile_cols, tile_count, cut_weights,
    send_idx, send_count, weight, bias, cotangent,
):
    rows, width = features.shape
    side = tile_vals.shape[1]
    blk = lax.axis_size("blk")
    dom = lax.axis_size("dom")
    slots = tile_vals.shape[0] // blk
    cuts = send_idx.shape[1]
    most = cuts // dom
    hidden = weight.shape[1]
    smem = pl.BlockSpec(memory_space=pltpu.SMEM)
    vmem = pl.BlockSpec(memory_space=pltpu.VMEM)
    whole = lambda *shape: pl.BlockSpec(shape, lambda s: (0,) * len(shape))
    a, picks, outgoing = pl.pallas_call(
        build,
        grid=(blk,),
        out_shape=(
            jax.ShapeDtypeStruct((blk, rows, rows), BF16),
            jax.ShapeDtypeStruct((rows, cuts), BF16),
            jax.ShapeDtypeStruct((dom, most, width), BF16),
        ),
        in_specs=[smem, smem, smem, smem,
                  pl.BlockSpec((slots, side, side), lambda s: (s, 0, 0)),
                  whole(1, cuts), whole(rows, width)],
        out_specs=(pl.BlockSpec((1, rows, rows), lambda s: (s, 0, 0)),
                   whole(rows, cuts), whole(dom, most, width)),
        compiler_params=pltpu.CompilerParams(vmem_limit_bytes=60 << 20),
    )(tile_count, tile_rows, tile_cols, send_count, tile_vals, send_idx, features)

    share = width // dom
    piece = share + 8
    dma = pltpu.SemaphoreType.DMA
    over_d, over_b = dma((dom,)), dma((blk,))
    hbm = pl.BlockSpec(memory_space=pl.ANY)
    shapes = (
        jax.ShapeDtypeStruct((rows, hidden), BF16),
        jax.ShapeDtypeStruct((rows, width), BF16),
        jax.ShapeDtypeStruct((width, hidden), F32),
        jax.ShapeDtypeStruct((1, hidden), F32),
    )
    results = pl.pallas_call(
        functools.partial(layer, dom, blk, 1.0 / math.sqrt(dom * blk * rows)),
        out_shape=shapes,
        in_specs=[hbm, vmem, hbm, hbm, vmem, hbm, vmem, hbm],
        out_specs=(vmem,) * 4,
        scratch_shapes=[
            pltpu.VMEM((blk, rows, rows), BF16),
            pltpu.VMEM((rows, cuts), BF16),
            pltpu.VMEM((rows, cuts), BF16),
            pltpu.VMEM((width, hidden), BF16),
            pltpu.VMEM((rows, hidden), BF16),
            pltpu.VMEM((blk, rows, width), BF16),
            pltpu.VMEM((dom, most, width), BF16),
            pltpu.VMEM((dom, most, width), BF16),
            pltpu.VMEM((dom, most, width), BF16),
            pltpu.VMEM((blk, width, rows), BF16),
            pltpu.VMEM((blk, width, rows), BF16),
            pltpu.VMEM((blk, width, rows), BF16),
            pltpu.VMEM((rows, width), F32),
            pltpu.VMEM((rows, width), BF16),
            pltpu.VMEM((rows, hidden), BF16),
            pltpu.VMEM((dom, piece, hidden), F32),
            pltpu.VMEM((dom, piece, hidden), F32),
            pltpu.VMEM((piece, hidden), F32),
            pltpu.VMEM((blk, piece, hidden), F32),
            pltpu.VMEM((dom, piece, hidden), F32),
            over_b, dma((4,)), over_b, over_b, over_b, over_b, over_d, over_d, over_d, over_d,
            over_b, over_b, over_b, over_b, over_d, over_d, over_b, over_b, over_d, over_d,
        ],
        compiler_params=pltpu.CompilerParams(
            collective_id=0, has_side_effects=True, vmem_limit_bytes=60 << 20
        ),
    )(a, features, cut_weights, picks, outgoing, weight, bias.reshape(1, hidden), cotangent)
    y, grad_x, grad_w, grad_b = pl.pallas_call(
        deliver,
        out_shape=shapes,
        in_specs=[vmem] * 4,
        out_specs=(vmem,) * 4,
        compiler_params=pltpu.CompilerParams(vmem_limit_bytes=60 << 20),
    )(*results)
    return y, grad_x, grad_w, grad_b.reshape(hidden)


def solution(mesh):
    split = P(("dom", "blk"), None)
    in_specs = (
        split, P(("dom", "blk"), None, None), split, split, split, split, split, split,
        P(), P(), split,
    )
    out_specs = (split, split, P(), P())
    return jax.shard_map(shards, mesh=mesh, in_specs=in_specs, out_specs=out_specs, check_vma=False)
```
